512 devices in a mesh: blk: 32 (over z, y_lo), uly: 16 (over x, y_hi, core).
Axes of the slice: x: 4, y: 8 (y_hi: 2, y_lo: 4; y = y_hi * 4 + y_lo), z: 8, core: 2. Of those that a mesh axis runs over, the one named last changes fastest.
Arguments:
- span_q: bfloat16 [1024, 4096], P(('blk', 'uly')), may hold values from -9 to 9
- span_k: bfloat16 [1024, 4096], P(('blk', 'uly')), may hold values from -9 to 9
- span_v: bfloat16 [1024, 4096], P(('blk', 'uly')), may hold values from -6 to 6
- span_grad: bfloat16 [1024, 4096], P(('blk', 'uly')), may hold values from -6 to 6
- mem_k: bfloat16 [31744, 4096], P(('blk', 'uly')), may hold values from -6 to 6
- mem_v: bfloat16 [31744, 4096], P(('blk', 'uly')), may hold values from -6 to 6
- retrieved: int32 [2, 32], replicated, may hold values from 0 to 61, all different within a row
- tile_keep: int32 [2, 248], replicated, may hold values 0 or 1
Outputs:
- grad_q: float32 [1024, 4096], P(('blk', 'uly'))
- grad_k: float32 [1024, 4096], P(('blk', 'uly'))
- grad_v: float32 [1024, 4096], P(('blk', 'uly'))
- grad_mem_k: float32 [31744, 4096], P(('blk', 'uly'))
- grad_mem_v: float32 [31744, 4096], P(('blk', 'uly'))
The draws below stay inside these ranges and needn't reach their ends.
Inputs may be any that keep to these rules, and one draw needn't show every extreme that they name: `retrieved`: each row names 32 different past frames, and every past frame is named by some row.
All inputs are finite; a program needn't handle non-finite values.
Results may differ from the reference program's by a relative error of at most 0.0047.
Values may be sent and summed in bfloat16 or wider, within the bound.
No kernel may reach another device: no remote copies, remote signals or barrier semaphores. Data moves between devices by JAX's collectives and lax.ppermute only.
A program may use at most 64 MiB of HBM per device.

```python
import math
import jax
import jax.numpy as jnp
from jax import lax

H = 32
DH = 128
QF = 2
MF = 62
R = 32
FT = 4
SPAN = 1024
MEM = 31744
FRAME = 512
TILE = 128
HD = 4096


def draw_span_q(key, part):
    key = jax.random.fold_in(key, 11)
    base_draw = jnp.clip(jax.random.normal(key, (SPAN, H * DH), jnp.float32), -6.0, 6.0)
    return base_draw.astype(jnp.bfloat16)


def draw_span_k(key, part):
    key = jax.random.fold_in(key, 23)
    base_draw = jnp.clip(jax.random.normal(key, (SPAN, H * DH), jnp.float32), -6.0, 6.0)
    return base_draw.astype(jnp.bfloat16)


def set_ends(values, stream_key, low, largest):
    shape = values.shape
    place = [jax.random.randint(jax.random.fold_in(stream_key, axis), (), 0, shape[axis]) for axis in range(len(shape))]
    values = values.at[tuple(place)].set(low)
    longest = shape.index(max(shape))
    place[longest] = (place[longest] + 1) % shape[longest]
    return values.at[tuple(place)].set(largest)


def levels(rng, dims, pieces, smallest, high):
    gain = 1.0
    for dim, shards_of in pieces:
        draws = jax.random.uniform(jax.random.fold_in(jax.random.fold_in(rng, 6), dim), (shards_of,), jnp.float32, smallest / len(pieces), high / len(pieces))
        gain = gain * jnp.repeat(jnp.exp(draws), dims[dim] // shards_of).reshape((-1,) + (1,) * (len(dims) - 1 - dim))
    return gain


def distinct(rng, rows, amount, top, lift):
    ranking = jax.random.permutation(jax.random.fold_in(rng, 1), amount)
    pull = ranking
    for power in range(3):
        pull = pull * pull // amount
    pull = pull * lift // amount
    lots = jax.random.randint(jax.random.fold_in(rng, 2), (rows, amount), 0, 4096) + pull
    sure = jax.random.permutation(jax.random.fold_in(rng, 3), rows)[jnp.arange(amount) % rows]
    lots = jnp.where(jnp.arange(rows)[:, None] == sure[None, :], 1 << 14, lots)
    priority = lots * amount + jnp.arange(amount)
    return lax.top_k(priority.astype(jnp.int32), top)[1].astype(jnp.int32)


def gaussian(rng, extent, deviation, bound, cuts=(), kind=jnp.bfloat16):
    loudness = levels(rng, extent, cuts, -0.22, 0.18) if cuts else 1.0
    result = jax.random.normal(rng, extent, jnp.float32) * deviation * loudness
    return jnp.minimum(jnp.maximum(result, -bound), bound).astype(kind)


def setup_inputs(seed: int = 0) -> dict:
    keys = jax.random.split(jax.random.key(seed), 9)
    return {
        "span_q": draw_span_q(jax.random.fold_in(keys[8], 71), 0),
        "span_k": draw_span_k(jax.random.fold_in(keys[8], 71), 0),
        "span_v": gaussian(keys[2], (SPAN, HD), 1.0, 6.0, ((0, 512),)),
        "span_grad": gaussian(keys[3], (SPAN, HD), 1.0, 6.0, ((0, 512),)),
        "mem_k": gaussian(keys[4], (MEM, HD), 1.0, 6.0, ((0, 512),)),
        "mem_v": gaussian(keys[5], (MEM, HD), 1.0, 6.0, ((0, 512),)),
        "retrieved": distinct(keys[6], QF, MF, R, 8456),
        "tile_keep": set_ends((jax.random.randint(keys[7], (QF, MF * FT), 0, 4) < 3).astype(jnp.int32), jax.random.fold_in(keys[7], 1), 0, 1),
    }


def allowed_mask(retrieved, tile_keep):
    query_frame = jnp.arange(SPAN, dtype=jnp.int32) // FRAME
    memory_index = jnp.arange(MEM, dtype=jnp.int32)
    frame_ids = jnp.arange(MF, dtype=jnp.int32)
    chosen = jnp.any(retrieved[:, :, None] == frame_ids[None, None, :], axis=1)
    frame_table = chosen[:, memory_index // FRAME] & (tile_keep[:, memory_index // TILE] == 1)
    memory_ok = frame_table[query_frame]
    own_ok = query_frame[None, :] <= query_frame[:, None]
    return jnp.concatenate([memory_ok, own_ok], axis=1)

def split_heads(array):
    return array.reshape(array.shape[0], H, DH).transpose(1, 0, 2)

def join_heads(array):
    return array.transpose(1, 0, 2).reshape(array.shape[1], H * DH)

def reference(span_q, span_k, span_v, span_grad, mem_k, mem_v, retrieved, tile_keep):
    permitted = allowed_mask(retrieved, tile_keep)
    score_scale = 1.0 / math.sqrt(DH)
    all_keys = split_heads(jnp.concatenate([mem_k, span_k], axis=0))
    all_values = split_heads(jnp.concatenate([mem_v, span_v], axis=0))

    def one_head(inputs):
        query_h, key_h, value_h, grad_h = inputs
        scores = jnp.dot(query_h, key_h.T, preferred_element_type=jnp.float32) * score_scale
        scores = jnp.where(permitted, scores, -jnp.inf)
        row_max = lax.optimization_barrier(jnp.max(scores, axis=1, keepdims=True))
        row_sum = lax.optimization_barrier(jnp.sum(jnp.exp(scores - row_max), axis=1, keepdims=True))
        log_total = row_max + jnp.log(row_sum)
        probs = jnp.exp(scores - log_total)
        products = jnp.dot(grad_h, value_h.T, preferred_element_type=jnp.float32)
        row_delta = lax.optimization_barrier(jnp.sum(probs * products, axis=1, keepdims=True))
        dscore = (probs * (products - row_delta)).astype(jnp.bfloat16)
        grad_query = jnp.dot(dscore, key_h, preferred_element_type=jnp.float32) * score_scale
        grad_key = jnp.dot(dscore.T, query_h, preferred_element_type=jnp.float32) * score_scale
        grad_value = jnp.dot(probs.astype(jnp.bfloat16).T, grad_h, preferred_element_type=jnp.float32)
        return (grad_query, grad_key, grad_value)
    grad_query, grad_key, grad_value = lax.map(one_head, (split_heads(span_q), all_keys, all_values, split_heads(span_grad)))
    grad_query = join_heads(grad_query)
    grad_key = join_heads(grad_key)
    grad_value = join_heads(grad_value)
    return (grad_query, grad_key[MEM:], grad_value[MEM:], grad_key[:MEM], grad_value[:MEM])
```

```python
import math

import jax
import jax.numpy as jnp
from jax import lax
from jax.experimental import pallas as pl
from jax.experimental.pallas import tpu as pltpu
from jax.sharding import Mesh, PartitionSpec as P

DH = 128
HEADS = 32
QF = 2
MF = 62
FT = 4
FRAME = 512
TILE = 128
MEM_ROWS = 62
SPAN_ROWS = 2
ROWS = MEM_ROWS + SPAN_ROWS

FINE = (("zh", 4), ("zl", 2), ("ym", 2), ("yl", 2), ("x", 4), ("yh", 2), ("core", 2))
NAMES = tuple(name for name, _ in FINE)
SIZES = tuple(size for _, size in FINE)
HEAD_AXES = ("zl", "yl", "x", "core")
KEY_AXES = ("zh", "ym", "yh")
GROUPS = 16

HALF = FRAME // HEADS
CHUNK = 512
SOURCES = CHUNK // ROWS
K_AT, V_AT, Q_AT, G_AT = 0, ROWS, 2 * ROWS, 2 * ROWS + 2 * HALF
SENT = 2 * ROWS + 4 * HALF
BACK = 2 * ROWS + 2 * HALF
WIDE = HEADS * DH // 2
LOG2E = math.log2(math.e)
SCALE = 1.0 / math.sqrt(DH)
BARRED = -1e30
FLOOR = -1e20


def load_queries(in_ref, qt_ref, gt_ref):
    pick = lax.broadcasted_iota(jnp.int32, (DH, FRAME), 0)
    for f in range(QF):
        q = in_ref[:, Q_AT + f * HALF : Q_AT + (f + 1) * HALF, :].reshape(FRAME, DH)
        g = in_ref[:, G_AT + f * HALF : G_AT + (f + 1) * HALF, :].reshape(FRAME, DH)
        qt_ref[f, 0:DH, :] = q.T
        qt_ref[f, DH : 2 * DH, :] = jnp.where(pick == f, 1.0, 0.0).astype(jnp.bfloat16)
        gt_ref[f] = g.T


def load_keys(in_ref, mask_ref, c):
    sources = pl.ds(c * SOURCES, SOURCES)
    keys = in_ref[sources, K_AT : K_AT + ROWS, :].reshape(CHUNK, DH)
    values = in_ref[sources, V_AT : V_AT + ROWS, :].reshape(CHUNK, DH)
    start = pl.multiple_of(c * CHUNK, CHUNK)
    masked_keys = jnp.concatenate([keys, mask_ref[pl.ds(start, CHUNK), :]], axis=1)
    return keys, masked_keys, values


def dot(a, b):
    return jnp.dot(a, b, preferred_element_type=jnp.float32)


def stats_kernel(in_ref, mask_ref, out_ref, qt_ref, gt_ref, max_ref, sum_ref, dot_ref):
    load_queries(in_ref, qt_ref, gt_ref)
    max_ref[...] = jnp.full(max_ref.shape, FLOOR, jnp.float32)
    sum_ref[...] = jnp.zeros(sum_ref.shape, jnp.float32)
    dot_ref[...] = jnp.zeros(dot_ref.shape, jnp.float32)

    def visit(c, carry):
        _, masked_keys, values = load_keys(in_ref, mask_ref, c)
        for f in range(QF):
            scores = (dot(masked_keys, qt_ref[f]) * (SCALE * LOG2E)).reshape(CHUNK // 8, 8, FRAME)
            products = dot(values, gt_ref[f]).reshape(CHUNK // 8, 8, FRAME)
            old = max_ref[f]
            new = jnp.maximum(old, jnp.max(scores, axis=0))
            weights = jnp.exp2(scores - new[None])
            rescale = jnp.exp2(old - new)
            max_ref[f] = new
            sum_ref[f] = sum_ref[f] * rescale + jnp.sum(weights, axis=0)
            dot_ref[f] = dot_ref[f] * rescale + jnp.sum(weights * products, axis=0)
        return carry

    lax.fori_loop(0, HEADS * ROWS // CHUNK, visit, 0)
    logs, means = [], []
    for f in range(QF):
        top = jnp.max(max_ref[f], axis=0, keepdims=True)
        rescale = jnp.exp2(max_ref[f] - top)
        total = jnp.sum(sum_ref[f] * rescale, axis=0, keepdims=True)
        inner = jnp.sum(dot_ref[f] * rescale, axis=0, keepdims=True)
        some = total > 0.0
        safe = jnp.where(some, total, 1.0)
        log_row = jnp.where(some, top + jnp.log(safe) * LOG2E, BARRED)
        mean_row = inner / safe
        logs += [log_row[:, :256], log_row[:, 256:]]
        means += [mean_row[:, :256], mean_row[:, 256:]]
    stats = jnp.concatenate(logs + means, axis=0)
    out_ref[...] = jnp.broadcast_to(stats[None], out_ref.shape)


def grads_kernel(in_ref, mask_ref, stats_ref, out_ref, qt_ref, gt_ref, acc_ref):
    load_queries(in_ref, qt_ref, gt_ref)
    acc_ref[...] = jnp.zeros(acc_ref.shape, jnp.float32)
    logs = stats_ref[:, 0:4, :]
    means = stats_ref[:, 4:8, :]
    top = jnp.max(logs, axis=0)
    weights = jnp.exp2(logs - top[None])
    total = jnp.sum(weights, axis=0)
    log_total = top + jnp.log(total) * LOG2E
    delta = jnp.sum(weights * means, axis=0) / total

    def row(stat, f):
        return jnp.concatenate([stat[2 * f : 2 * f + 1], stat[2 * f + 1 : 2 * f + 2]], axis=1)

    log_rows = [row(log_total, f) for f in range(QF)]
    delta_rows = [row(delta, f) for f in range(QF)]

    def visit(c, carry):
        keys, masked_keys, values = load_keys(in_ref, mask_ref, c)
        keys_t = keys.T
        key_grad = jnp.zeros((CHUNK, DH), jnp.float32)
        value_grad = jnp.zeros((CHUNK, DH), jnp.float32)
        for f in range(QF):
            q = in_ref[:, Q_AT + f * HALF : Q_AT + (f + 1) * HALF, :].reshape(FRAME, DH)
            g = in_ref[:, G_AT + f * HALF : G_AT + (f + 1) * HALF, :].reshape(FRAME, DH)
            scores = dot(masked_keys, qt_ref[f]) * (SCALE * LOG2E)
            probs = jnp.exp2(scores - log_rows[f])
            products = dot(values, gt_ref[f])
            dscore = (probs * (products - delta_rows[f])).astype(jnp.bfloat16)
            value_grad += dot(probs.astype(jnp.bfloat16), g)
            key_grad += dot(dscore, q)
            acc_ref[f] += dot(keys_t, dscore)
        sources = pl.ds(c * SOURCES, SOURCES)
        out_ref[sources, K_AT : K_AT + ROWS, :] = (
            (key_grad * SCALE).astype(jnp.bfloat16).reshape(SOURCES, ROWS, DH)
        )
        out_ref[sources, V_AT : V_AT + ROWS, :] = value_grad.astype(jnp.bfloat16).reshape(
            SOURCES, ROWS, DH
        )
        return carry

    lax.fori_loop(0, HEADS * ROWS // CHUNK, visit, 0)
    for f in range(QF):
        query_grad = (acc_ref[f].T * SCALE).astype(jnp.bfloat16)
        out_ref[:, Q_AT + f * HALF : Q_AT + (f + 1) * HALF, :] = query_grad.reshape(HEADS, HALF, DH)


def mask_rows(retrieved, tile_keep):
    tiles = jnp.arange(256, dtype=jnp.int32)
    chosen = jnp.any(retrieved[:, :, None] == (tiles // FT)[None, None, :], axis=1)
    kept = jnp.pad(tile_keep, ((0, 0), (0, 256 - MF * FT))) == 1
    own = (tiles[None, :] >= MF * FT) & (
        tiles[None, :] - MF * FT <= jnp.arange(QF, dtype=jnp.int32)[:, None]
    )
    barred = 1.0 - ((chosen & kept) | own).astype(jnp.float32)
    barred = jnp.pad(barred, ((0, DH - QF), (0, 0)))
    row = jnp.arange(HEADS * ROWS, dtype=jnp.int32)
    source, inner = row // ROWS, row % ROWS
    place = {"core": source % 2, "x": source // 2 % 4, "yl": source // 8 % 2, "zl": source // 16}
    device = 0
    for name, size in FINE:
        device = device * size + (place[name] if name in place else lax.axis_index(name))
    tile = jnp.where(
        inner < MEM_ROWS,
        (device * MEM_ROWS + inner) // TILE,
        MF * FT + (device * SPAN_ROWS + inner - MEM_ROWS) // FRAME,
    )
    onehot = (tile[:, None] == tiles[None, :]).astype(jnp.float32)
    hit = lax.dot_general(onehot, barred, (((1,), (1,)), ((), ())))
    return jnp.where(hit > 0.5, BARRED, 0.0).astype(jnp.bfloat16)


def spread_kernel(q_ref, g_ref, out_ref):
    rows = jnp.concatenate(
        [part[:, half] for part in (q_ref, g_ref) for half in (slice(0, WIDE), slice(WIDE, 2 * WIDE))],
        axis=0,
    )
    for b in range(0, GROUPS, 2):
        out_ref[8 * b : 8 * (b + 2), :] = jnp.concatenate([rows, rows], axis=0)


def moved(order, rows):
    count = rows.shape[0]
    to = lax.broadcasted_iota(jnp.int32, (count, count), 0)
    at = lax.broadcasted_iota(jnp.int32, (count, count), 1)
    pick = jnp.where(order(to) == at, 1.0, 0.0).astype(jnp.bfloat16)
    return dot(pick, rows).astype(jnp.bfloat16)


def pack_kernel(gathered_ref, mem_k_ref, span_k_ref, mem_v_ref, span_v_ref, out_ref):
    rows = moved(
        lambda i: (i // 2 % 16) * 8 + (i // 32 % 2) * 4 + (i // 64) * 2 + i % 2, gathered_ref[...]
    )
    for h in range(HEADS):
        lanes = slice(h * DH, (h + 1) * DH)
        out_ref[h, K_AT : K_AT + MEM_ROWS, :] = mem_k_ref[:, lanes]
        out_ref[h, K_AT + MEM_ROWS : K_AT + ROWS, :] = span_k_ref[:, lanes]
        out_ref[h, V_AT : V_AT + MEM_ROWS, :] = mem_v_ref[:, lanes]
        out_ref[h, V_AT + MEM_ROWS : V_AT + ROWS, :] = span_v_ref[:, lanes]
        half, at = divmod(h * DH, WIDE)
        out_ref[h, Q_AT:SENT, :] = rows[half * 4 * HALF : (half + 1) * 4 * HALF, at : at + DH]


def unpack_queries_kernel(back_ref, out_ref):
    quarters = []
    for quarter in range(4):
        heads = [back_ref[quarter * 8 + i, Q_AT:BACK, :] for i in range(8)]
        quarters.append(jnp.concatenate(heads, axis=1))
    rows = jnp.concatenate(quarters, axis=0)
    out_ref[...] = moved(lambda i: (i // 2 % 4) * 32 + (i // 8) * 2 + i % 2, rows)


def unpack_keys_kernel(back_ref, mem_k_ref, mem_v_ref, span_k_ref, span_v_ref):
    for h in range(HEADS):
        lanes = slice(h * DH, (h + 1) * DH)
        key_grad = back_ref[h, K_AT : K_AT + ROWS, :].astype(jnp.float32)
        value_grad = back_ref[h, V_AT : V_AT + ROWS, :].astype(jnp.float32)
        mem_k_ref[:, lanes] = key_grad[:MEM_ROWS]
        mem_v_ref[:, lanes] = value_grad[:MEM_ROWS]
        span_k_ref[:, lanes] = key_grad[MEM_ROWS:]
        span_v_ref[:, lanes] = value_grad[MEM_ROWS:]


def call(kernel, name, out_shape, scratch_shapes=(), flops=0, transcendentals=0, moved_bytes=2 << 20):
    return pl.pallas_call(
        kernel,
        out_shape=out_shape,
        scratch_shapes=list(scratch_shapes),
        compiler_params=pltpu.CompilerParams(vmem_limit_bytes=40 * 1024 * 1024),
        cost_estimate=pl.CostEstimate(
            flops=flops, bytes_accessed=moved_bytes, transcendentals=transcendentals
        ),
        name=name,
    )


def shape(dims, dtype):
    return jax.ShapeDtypeStruct(dims, dtype)


def local(span_q, span_k, span_v, span_grad, mem_k, mem_v, retrieved, tile_keep):
    bf16, f32 = jnp.bfloat16, jnp.float32
    pairs = HEADS * ROWS * QF * FRAME
    queries = [pltpu.VMEM((QF, 2 * DH, FRAME), bf16), pltpu.VMEM((QF, DH, FRAME), bf16)]
    sums = [pltpu.VMEM((QF, 8, FRAME), f32)] * 3

    spread = call(spread_kernel, "spread", shape((8 * GROUPS, WIDE), bf16))(span_q, span_grad)
    gathered = lax.all_to_all(spread, KEY_AXES, 0, 0, tiled=True)
    packed = call(pack_kernel, "pack", shape((HEADS, SENT, DH), bf16))(
        gathered, mem_k, span_k, mem_v, span_v
    )
    held = lax.all_to_all(packed, HEAD_AXES, 0, 0, tiled=True)

    mask = mask_rows(retrieved, tile_keep)
    stats = call(
        stats_kernel,
        "stats",
        shape((GROUPS, 8, 256), f32),
        queries + sums,
        flops=6 * pairs * DH,
        transcendentals=pairs,
    )(held, mask)
    stats = lax.all_to_all(stats, KEY_AXES, 0, 0, tiled=True)
    grads = call(
        grads_kernel,
        "grads",
        shape((HEADS, BACK, DH), bf16),
        queries + [pltpu.VMEM((QF, DH, FRAME), f32)],
        flops=12 * pairs * DH,
        transcendentals=pairs,
    )(held, mask, stats)

    back = lax.all_to_all(grads, HEAD_AXES, 0, 0, tiled=True)
    parts = call(unpack_queries_kernel, "unpack_queries", shape((8 * GROUPS, WIDE // 2), bf16))(back)
    parts = lax.all_to_all(parts, KEY_AXES, 0, 0, tiled=True)
    grad_mem_k, grad_mem_v, grad_k, grad_v = call(
        unpack_keys_kernel,
        "unpack_keys",
        (shape((MEM_ROWS, HEADS * DH), f32),) * 2 + (shape((SPAN_ROWS, HEADS * DH), f32),) * 2,
        moved_bytes=4 << 20,
    )(back)
    grad_q = jnp.sum(parts.reshape(GROUPS, 4, SPAN_ROWS, WIDE // 2).astype(f32), axis=0)
    grad_q = grad_q.transpose(1, 0, 2).reshape(SPAN_ROWS, HEADS * DH)
    return grad_q, grad_k, grad_v, grad_mem_k, grad_mem_v


def solution(mesh):
    fine = Mesh(mesh.devices.reshape(SIZES), NAMES)
    rows = P(NAMES, None)
    return jax.shard_map(
        local,
        mesh=fine,
        in_specs=(rows,) * 6 + (P(), P()),
        out_specs=(rows,) * 5,
        check_vma=False,
    )
```

```python
import functools
import math

import jax
import jax.numpy as jnp
from jax import lax
from jax.experimental import pallas as pl
from jax.experimental.pallas import tpu as pltpu
from jax.sharding import Mesh, PartitionSpec as P

DH = 128
HEADS = 32
QF = 2
MF = 62
FT = 4
FRAME = 512
TILE = 128
MEM_ROWS = 62
SPAN_ROWS = 2
ROWS = MEM_ROWS + SPAN_ROWS

FINE = (("zh", 4), ("zl", 2), ("ym", 2), ("yl", 2), ("x", 4), ("yh", 2), ("core", 2))
NAMES = tuple(name for name, _ in FINE)
SIZES = tuple(size for _, size in FINE)
HEAD_AXES = ("zl", "yl", "x", "core")
KEY_AXES = ("zh", "ym", "yh")
GROUPS = 16
HALF_GROUPS = GROUPS // QF
NEAR_AXES, NEAR = ("ym", "yh"), 4
FAR_AXES, FAR = ("zh",), 4

HALF = FRAME // HEADS
CHUNK = 512
SOURCES = CHUNK // ROWS
BLOCK = HEADS * SPAN_ROWS
K_AT, V_AT, Q_AT = 0, ROWS, 2 * ROWS
SENT = 2 * ROWS
BACK = 2 * ROWS + 2 * HALF
WIDE = HEADS * DH // 2
LOG2E = math.log2(math.e)
SCALE = 1.0 / math.sqrt(DH)
BARRED = -1e30
FLOOR = -1e20


def load_queries(qg_ref, qt_ref, gt_ref):
    pick = lax.broadcasted_iota(jnp.int32, (DH, FRAME), 0)
    for f in range(QF):
        qt_ref[f, 0:DH, :] = frame_rows(qg_ref, 0, f).T
        qt_ref[f, DH : 2 * DH, :] = jnp.where(pick == f, 1.0, 0.0).astype(jnp.bfloat16)
        gt_ref[f] = frame_rows(qg_ref, 1, f).T


def frame_rows(qg_ref, which, f):
    return qg_ref[which, f * HALF_GROUPS : (f + 1) * HALF_GROUPS, :, :].reshape(FRAME, DH)


def load_keys(in_ref, mask_ref, c):
    sources = pl.ds(c * SOURCES, SOURCES)
    keys = in_ref[sources, K_AT : K_AT + ROWS, :].reshape(CHUNK, DH)
    values = in_ref[sources, V_AT : V_AT + ROWS, :].reshape(CHUNK, DH)
    start = pl.multiple_of(c * CHUNK, CHUNK)
    masked_keys = jnp.concatenate([keys, mask_ref[pl.ds(start, CHUNK), :]], axis=1)
    return keys, masked_keys, values


def dot(a, b):
    return jnp.dot(a, b, preferred_element_type=jnp.float32)


def stats_kernel(group_ref, in_ref, mask_ref, *refs):
    blocks = refs[:FAR]
    out_ref, qg_ref, qt_ref, gt_ref, max_ref, sum_ref, dot_ref = refs[FAR:]
    for j in range(GROUPS):
        group = group_ref[0] ^ j
        qg_ref[0, group] = blocks[j // NEAR][j % NEAR, :BLOCK, :]
        qg_ref[1, group] = blocks[j // NEAR][j % NEAR, BLOCK:, :]
    load_queries(qg_ref, qt_ref, gt_ref)
    max_ref[...] = jnp.full(max_ref.shape, FLOOR, jnp.float32)
    sum_ref[...] = jnp.zeros(sum_ref.shape, jnp.float32)
    dot_ref[...] = jnp.zeros(dot_ref.shape, jnp.float32)

    def visit(c, carry):
        _, masked_keys, values = load_keys(in_ref, mask_ref, c)
        for f in range(QF):
            scores = (dot(masked_keys, qt_ref[f]) * (SCALE * LOG2E)).reshape(CHUNK // 8, 8, FRAME)
            products = dot(values, gt_ref[f]).reshape(CHUNK // 8, 8, FRAME)
            old = max_ref[f]
            new = jnp.maximum(old, jnp.max(scores, axis=0))
            weights = jnp.exp2(scores - new[None])
            rescale = jnp.exp2(old - new)
            max_ref[f] = new
            sum_ref[f] = sum_ref[f] * rescale + jnp.sum(weights, axis=0)
            dot_ref[f] = dot_ref[f] * rescale + jnp.sum(weights * products, axis=0)
        return carry

    lax.fori_loop(0, HEADS * ROWS // CHUNK, visit, 0)
    logs, means = [], []
    for f in range(QF):
        top = jnp.max(max_ref[f], axis=0, keepdims=True)
        rescale = jnp.exp2(max_ref[f] - top)
        total = jnp.sum(sum_ref[f] * rescale, axis=0, keepdims=True)
        inner = jnp.sum(dot_ref[f] * rescale, axis=0, keepdims=True)
        some = total > 0.0
        safe = jnp.where(some, total, 1.0)
        log_row = jnp.where(some, top + jnp.log(safe) * LOG2E, BARRED)
        mean_row = inner / safe
        logs += [log_row[:, :256], log_row[:, 256:]]
        means += [mean_row[:, :256], mean_row[:, 256:]]
    out_ref[...] = jnp.concatenate(logs + means, axis=0)


def merged(stats_refs):
    logs = [ref[0:4, :] for ref in stats_refs]
    top = functools.reduce(jnp.maximum, logs)
    weights = [jnp.exp2(log - top) for log in logs]
    total = sum(weights)
    means = sum(weight * ref[4:8, :] for weight, ref in zip(weights, stats_refs))
    return top + jnp.log(total) * LOG2E, means / total


def merge_kernel(*refs):
    log_total, mean = merged(refs[:-1])
    refs[-1][...] = jnp.concatenate([log_total, mean], axis=0)


def grads_kernel(in_ref, mask_ref, qg_ref, *refs):
    stats_refs = refs[:FAR]
    out_ref, qt_ref, gt_ref, acc_ref = refs[FAR:]
    load_queries(qg_ref, qt_ref, gt_ref)
    acc_ref[...] = jnp.zeros(acc_ref.shape, jnp.float32)
    log_total, delta = merged(stats_refs)

    def row(stat, f):
        return jnp.concatenate([stat[2 * f : 2 * f + 1], stat[2 * f + 1 : 2 * f + 2]], axis=1)

    log_rows = [row(log_total, f) for f in range(QF)]
    delta_rows = [row(delta, f) for f in range(QF)]

    def visit(c, carry):
        keys, masked_keys, values = load_keys(in_ref, mask_ref, c)
        keys_t = keys.T
        key_grad = jnp.zeros((CHUNK, DH), jnp.float32)
        value_grad = jnp.zeros((CHUNK, DH), jnp.float32)
        for f in range(QF):
            q, g = frame_rows(qg_ref, 0, f), frame_rows(qg_ref, 1, f)
            scores = dot(masked_keys, qt_ref[f]) * (SCALE * LOG2E)
            probs = jnp.exp2(scores - log_rows[f])
            products = dot(values, gt_ref[f])
            dscore = (probs * (products - delta_rows[f])).astype(jnp.bfloat16)
            value_grad += dot(probs.astype(jnp.bfloat16), g)
            key_grad += dot(dscore, q)
            acc_ref[f] += dot(keys_t, dscore)
        sources = pl.ds(c * SOURCES, SOURCES)
        out_ref[sources, K_AT : K_AT + ROWS, :] = (
            (key_grad * SCALE).astype(jnp.bfloat16).reshape(SOURCES, ROWS, DH)
        )
        out_ref[sources, V_AT : V_AT + ROWS, :] = value_grad.astype(jnp.bfloat16).reshape(
            SOURCES, ROWS, DH
        )
        return carry

    lax.fori_loop(0, HEADS * ROWS // CHUNK, visit, 0)
    for f in range(QF):
        query_grad = moved(
            lambda i: (i // 2 % HALF_GROUPS) * BLOCK + (i // HALF) * 2 + i % 2,
            (acc_ref[f] * SCALE).astype(jnp.bfloat16).T,
        )
        out_ref[:, Q_AT + f * HALF : Q_AT + (f + 1) * HALF, :] = query_grad.reshape(HEADS, HALF, DH)


def mask_rows(retrieved, tile_keep):
    tiles = jnp.arange(256, dtype=jnp.int32)
    chosen = jnp.any(retrieved[:, :, None] == (tiles // FT)[None, None, :], axis=1)
    kept = jnp.pad(tile_keep, ((0, 0), (0, 256 - MF * FT))) == 1
    own = (tiles[None, :] >= MF * FT) & (
        tiles[None, :] - MF * FT <= jnp.arange(QF, dtype=jnp.int32)[:, None]
    )
    barred = 1.0 - ((chosen & kept) | own).astype(jnp.float32)
    barred = jnp.pad(barred, ((0, DH - QF), (0, 0)))
    row = jnp.arange(HEADS * ROWS, dtype=jnp.int32)
    source, inner = row // ROWS, row % ROWS
    place = {"core": source % 2, "x": source // 2 % 4, "yl": source // 8 % 2, "zl": source // 16}
    device = 0
    for name, size in FINE:
        device = device * size + (place[name] if name in place else lax.axis_index(name))
    tile = jnp.where(
        inner < MEM_ROWS,
        (device * MEM_ROWS + inner) // TILE,
        MF * FT + (device * SPAN_ROWS + inner - MEM_ROWS) // FRAME,
    )
    onehot = (tile[:, None] == tiles[None, :]).astype(jnp.float32)
    hit = lax.dot_general(onehot, barred, (((1,), (1,)), ((), ())))
    return jnp.where(hit > 0.5, BARRED, 0.0).astype(jnp.bfloat16)


def split_kernel(q_ref, g_ref, out_ref):
    rows = jnp.concatenate([q_ref[...], g_ref[...], q_ref[...], g_ref[...]], axis=0)
    for h in range(HEADS):
        out_ref[h] = rows[:, h * DH : (h + 1) * DH]


def moved(order, rows, count=None):
    dims = (count or rows.shape[0], rows.shape[0])
    to = lax.broadcasted_iota(jnp.int32, dims, 0)
    at = lax.broadcasted_iota(jnp.int32, dims, 1)
    pick = jnp.where(order(to) == at, 1.0, 0.0).astype(jnp.bfloat16)
    return dot(pick, rows).astype(jnp.bfloat16)


def block_kernel(in_ref, out_ref):
    rows = in_ref[...].reshape(8 * HEADS, DH)
    out_ref[...] = moved(lambda i: (i // 2 % HEADS) * 8 + (i // BLOCK) * 2 + i % 2, rows, 2 * BLOCK)


def pack_kernel(mem_k_ref, span_k_ref, mem_v_ref, span_v_ref, out_ref):
    for h in range(HEADS):
        lanes = slice(h * DH, (h + 1) * DH)
        out_ref[h, K_AT : K_AT + MEM_ROWS, :] = mem_k_ref[:, lanes]
        out_ref[h, K_AT + MEM_ROWS : K_AT + ROWS, :] = span_k_ref[:, lanes]
        out_ref[h, V_AT : V_AT + MEM_ROWS, :] = mem_v_ref[:, lanes]
        out_ref[h, V_AT + MEM_ROWS : V_AT + ROWS, :] = span_v_ref[:, lanes]


def unpack_queries_kernel(back_ref, out_ref):
    quarters = []
    for quarter in range(4):
        heads = [back_ref[quarter * 8 + i, Q_AT:BACK, :] for i in range(8)]
        quarters.append(jnp.concatenate(heads, axis=1))
    rows = jnp.concatenate(quarters, axis=0)
    out_ref[...] = moved(lambda i: (i // 2 % 4) * 32 + (i // 8) * 2 + i % 2, rows)


def unpack_keys_kernel(back_ref, mem_k_ref, mem_v_ref, span_k_ref, span_v_ref):
    for h in range(HEADS):
        lanes = slice(h * DH, (h + 1) * DH)
        key_grad = back_ref[h, K_AT : K_AT + ROWS, :].astype(jnp.float32)
        value_grad = back_ref[h, V_AT : V_AT + ROWS, :].astype(jnp.float32)
        mem_k_ref[:, lanes] = key_grad[:MEM_ROWS]
        mem_v_ref[:, lanes] = value_grad[:MEM_ROWS]
        span_k_ref[:, lanes] = key_grad[MEM_ROWS:]
        span_v_ref[:, lanes] = value_grad[MEM_ROWS:]


def call(kernel, name, out_shape, scratch_shapes=(), flops=0, transcendentals=0, moved_bytes=2 << 20, scalars=0, arrays=1):
    return pl.pallas_call(
        kernel,
        in_specs=[pl.BlockSpec(memory_space=pltpu.SMEM)] * scalars
        + [pl.BlockSpec(memory_space=pltpu.VMEM)] * arrays,
        out_shape=out_shape,
        scratch_shapes=list(scratch_shapes),
        compiler_params=pltpu.CompilerParams(vmem_limit_bytes=40 * 1024 * 1024),
        cost_estimate=pl.CostEstimate(
            flops=flops, bytes_accessed=moved_bytes, transcendentals=transcendentals
        ),
        name=name,
    )


def swaps(array, axes, size):
    return [array] + [
        lax.ppermute(array, axes, [(i, i ^ j) for i in range(size)]) for j in range(1, size)
    ]


def shape(dims, dtype):
    return jax.ShapeDtypeStruct(dims, dtype)


def local(span_q, span_k, span_v, span_grad, mem_k, mem_v, retrieved, tile_keep):
    bf16, f32 = jnp.bfloat16, jnp.float32
    pairs = HEADS * ROWS * QF * FRAME
    queries = [pltpu.VMEM((QF, 2 * DH, FRAME), bf16), pltpu.VMEM((QF, DH, FRAME), bf16)]
    sums = [pltpu.VMEM((QF, 8, FRAME), f32)] * 3

    split = call(split_kernel, "split", shape((HEADS, 8, DH), bf16), arrays=2)(span_q, span_grad)
    split = lax.all_to_all(split, HEAD_AXES, 0, 0, tiled=True)
    block = call(block_kernel, "block", shape((2 * BLOCK, DH), bf16))(split)
    near = jnp.stack(swaps(block, NEAR_AXES, NEAR))
    blocks = swaps(near, FAR_AXES, FAR)
    packed = call(pack_kernel, "pack", shape((HEADS, SENT, DH), bf16), arrays=4)(
        mem_k, span_k, mem_v, span_v
    )
    held = lax.all_to_all(packed, HEAD_AXES, 0, 0, tiled=True)

    mask = mask_rows(retrieved, tile_keep)
    group = lax.axis_index(KEY_AXES).astype(jnp.int32).reshape(1)
    stats, queries_grads = call(
        stats_kernel,
        "stats",
        (shape((8, 256), f32), shape((2, GROUPS, BLOCK, DH), bf16)),
        queries + sums,
        flops=6 * pairs * DH,
        transcendentals=pairs,
        scalars=1,
        arrays=2 + FAR,
    )(group, held, mask, *blocks)
    near_stats = call(merge_kernel, "merge", shape((8, 256), f32), arrays=NEAR)(
        *swaps(stats, NEAR_AXES, NEAR)
    )
    all_stats = swaps(near_stats, FAR_AXES, FAR)
    grads = call(
        grads_kernel,
        "grads",
        shape((HEADS, BACK, DH), bf16),
        queries + [pltpu.VMEM((QF, DH, FRAME), f32)],
        flops=12 * pairs * DH,
        transcendentals=pairs,
        arrays=3 + FAR,
    )(held, mask, queries_grads, *all_stats)

    back = lax.all_to_all(grads, HEAD_AXES, 0, 0, tiled=True)
    parts = call(unpack_queries_kernel, "unpack_queries", shape((8 * GROUPS, WIDE // 2), bf16))(back)
    parts = lax.all_to_all(parts, KEY_AXES, 0, 0, tiled=True)
    grad_mem_k, grad_mem_v, grad_k, grad_v = call(
        unpack_keys_kernel,
        "unpack_keys",
        (shape((MEM_ROWS, HEADS * DH), f32),) * 2 + (shape((SPAN_ROWS, HEADS * DH), f32),) * 2,
        moved_bytes=4 << 20,
    )(back)
    grad_q = jnp.sum(parts.reshape(GROUPS, 4, SPAN_ROWS, WIDE // 2).astype(f32), axis=0)
    grad_q = grad_q.transpose(1, 0, 2).reshape(SPAN_ROWS, HEADS * DH)
    return grad_q, grad_k, grad_v, grad_mem_k, grad_mem_v


def solution(mesh):
    fine = Mesh(mesh.devices.reshape(SIZES), NAMES)
    rows = P(NAMES, None)
    return jax.shard_map(
        local,
        mesh=fine,
        in_specs=(rows,) * 6 + (P(), P()),
        out_specs=(rows,) * 5,
        check_vma=False,
    )
```
